128 devices in a mesh: tok: 8 (over z, y_hi), lat: 8 (over x, y_lo), src: 2 (over core).
Axes of the slice: x: 4, y: 4 (y_hi: 2, y_lo: 2; y = y_hi * 2 + y_lo), z: 4, core: 2. Of those that a mesh axis runs over, the one named last changes fastest.
Arguments:
- residuals: bfloat16 [2, 2048, 8192], P('src', 'tok', 'lat'), may hold values from -6 to 6
- enc_weight: bfloat16 [2, 8192, 16384], P('src', 'tok', 'lat'), may hold values from -0.046875 to 0.046875
- dec_weight: bfloat16 [2, 16384, 8192], P('src', 'lat', 'tok'), may hold values from -0.0625 to 0.0625
- enc_bias: float32 [16384], P('lat'), may hold values from -3 to 3
- dec_bias: float32 [2, 8192], P('src', 'tok'), may hold values from -3 to 3
- active: int32 [2048, 16384], P('tok', 'lat'), may hold values 0 or 1
Outputs:
- latent_codes: bfloat16 [2048, 16384], P('tok', 'lat')
- rebuilt: bfloat16 [2, 2048, 8192], P('src', 'lat', 'tok')
The draws below stay inside these ranges and needn't reach their ends.
Inputs may be any that keep to these rules, and one draw needn't show every extreme that they name: `active`: each entry is 0 or 1. The number of kept latents of a token, or of a device's block, has no bound below the full shape that may be relied on.
All inputs are finite; a program needn't handle non-finite values.
Results may differ from the reference program's by a relative error of at most 0.0045.
Values may be sent and summed in bfloat16 or wider, within the bound.
A program may use at most 128 MiB of HBM per device.

```python
import jax
import jax.numpy as jnp

D = 8192
LATENTS = 16384
TOKENS = 2048


def plant(array, stream_key, low, largest):
    longest = array.shape.index(max(array.shape))
    spots = []
    for shift in (0, 1):
        where = [jax.random.randint(jax.random.fold_in(stream_key, axis), (), 0, length) for axis, length in enumerate(array.shape)]
        where[longest] = (where[longest] + shift) % array.shape[longest]
        spots.append(tuple(where))
    return array.at[spots[0]].set(low).at[spots[1]].set(largest)


def levels(key, shape, split, least, high):
    factor_of, own = 1.0, jax.random.fold_in(key, 6)
    for position, parts in split:
        steps = jnp.exp(jax.random.uniform(jax.random.fold_in(own, position), (parts,), jnp.float32, least / len(split), high / len(split)))
        factor_of = factor_of * jnp.repeat(steps, shape[position] // parts).reshape([-1 if axis == position else 1 for axis in range(len(shape))])
    return factor_of


def centred(key, shape, width, bound, shards=(), dtype=jnp.bfloat16):
    drawn = width * jax.random.normal(key, shape, jnp.float32)
    if shards:
        drawn = drawn * levels(key, shape, shards, -0.22, 0.18)
    return jnp.clip(drawn, -bound, bound).astype(dtype)


def setup_inputs(seed: int = 0) -> dict:
    seeds = jax.random.split(jax.random.key(seed), 7)
    residuals = centred(seeds[0], (2, TOKENS, D), 1.0, 6.0, ((0, 2), (1, 8), (2, 8)))
    enc_weight = centred(seeds[1], (2, D, LATENTS), (2 * D) ** -0.5, 0.046875, ((0, 2), (1, 8), (2, 8)))
    dec_weight = centred(seeds[2], (2, LATENTS, D), (LATENTS // 2) ** -0.5, 0.0625, ((0, 2), (1, 8), (2, 8)))
    enc_bias = centred(seeds[3], (LATENTS,), 0.5, 3.0, ((0, 8),), jnp.float32)
    dec_bias = centred(seeds[4], (2, D), 0.5, 3.0, ((0, 2), (1, 8)), jnp.float32)
    active = plant((jax.random.randint(seeds[5], (TOKENS, LATENTS), 0, 4) < 3).astype(jnp.int32), jax.random.fold_in(seeds[5], 1), 0, 1)
    return dict(residuals=residuals, enc_weight=enc_weight, dec_weight=dec_weight, enc_bias=enc_bias, dec_bias=dec_bias, active=active)


def reference(residuals, enc_weight, dec_weight, enc_bias, dec_bias, active):
    preact = jnp.dot(residuals[0], enc_weight[0], preferred_element_type=jnp.float32)
    preact = preact + jnp.dot(residuals[1], enc_weight[1], preferred_element_type=jnp.float32)
    preact = preact + enc_bias[None, :]
    positive = jnp.maximum(preact, 0.0)
    latent_codes = jnp.where(active == 1, positive, 0.0).astype(jnp.bfloat16)
    first = jnp.dot(latent_codes, dec_weight[0], preferred_element_type=jnp.float32) + dec_bias[0][None, :]
    second = jnp.dot(latent_codes, dec_weight[1], preferred_element_type=jnp.float32) + dec_bias[1][None, :]
    rebuilt = jnp.stack([first, second]).astype(jnp.bfloat16)
    return latent_codes, rebuilt
```

```python
import jax
import jax.numpy as jnp
from jax import lax
from jax.experimental import pallas as pl
from jax.experimental.pallas import tpu as pltpu
from jax.sharding import PartitionSpec as P

PARTS = 8
RING = 4
BF16 = jnp.bfloat16
F32 = jnp.float32


class Group:
    def __init__(self, axis):
        self.axis = axis
        self.me = lax.axis_index(axis)
        self.ring = self.me // 2
        self.half = self.me % 2
        self.right = self.at(1, self.half)
        self.left = self.at(3, self.half)
        self.partner = self.at(0, 1 - self.half)

    def at(self, step, half):
        return 2 * ((self.ring + step) % RING) + half

    def neighbours(self):
        return [{self.axis: self.right}, {self.axis: self.left}, {self.axis: self.partner}]


class Gather:
    def __init__(self, group, buf, send, recv, sub):
        self.group, self.buf, self.send, self.recv, self.sub = group, buf, send, recv, sub

    def copy(self, q, block, message, to):
        rows = pl.ds(pl.multiple_of(block * self.sub, self.sub), self.sub)
        place = self.buf.at[q, rows, :]
        return pltpu.make_async_remote_copy(
            place, place, self.send.at[q, message], self.recv.at[q, message],
            device_id={self.group.axis: to},
        )

    def first(self, q):
        g = self.group
        self.copy(q, g.me, 1, g.right).start()
        self.copy(q, g.me, 2, g.left).start()
        self.copy(q, g.me, 0, g.partner).start()

    def second(self, q):
        g = self.group
        self.copy(q, g.left, 1, g.right).wait_recv()
        self.copy(q, g.left, 5, g.right).start()
        self.copy(q, g.partner, 0, g.partner).wait_recv()
        self.copy(q, g.partner, 4, g.left).start()
        self.copy(q, g.partner, 3, g.right).start()
        self.copy(q, g.right, 2, g.right).wait_recv()

    def third(self, q):
        g = self.group
        self.copy(q, g.at(1, 1 - g.half), 4, g.right).wait_recv()
        self.copy(q, g.at(1, 1 - g.half), 6, g.left).start()
        self.copy(q, g.at(3, 1 - g.half), 3, g.right).wait_recv()

    def last(self, q):
        g = self.group
        self.copy(q, g.at(2, g.half), 5, g.right).wait_recv()
        self.copy(q, g.at(2, 1 - g.half), 6, g.right).wait_recv()

    def drain(self, q):
        g = self.group
        for message in range(7):
            self.copy(q, g.me, message, g.right).wait_send()


class Scatter:
    def __init__(self, group, sums, place, out1, in1, out2, in2, out3, in3, keep, send, recv, sub):
        self.group, self.sums, self.place = group, sums, place
        self.out1, self.in1, self.out2, self.in2 = out1, in1, out2, in2
        self.out3, self.in3, self.keep = out3, in3, keep
        self.send, self.recv, self.sub = send, recv, sub

    def rows(self, q, owner):
        start = pl.multiple_of(self.place(q, owner) * self.sub, self.sub)
        return self.sums[q % 4, pl.ds(start, self.sub), :]

    def copy(self, q, message):
        g = self.group
        src, dst = {
            0: (self.out1.at[q, 0], self.in1.at[q, 0]),
            1: (self.out1.at[q, 1], self.in1.at[q, 1]),
            2: (self.out2.at[q, 0], self.in2.at[q, 0]),
            3: (self.out2.at[q, 1], self.in2.at[q, 1]),
            4: (self.out3.at[q], self.in3.at[q]),
        }[message]
        to = g.partner if message == 4 else (g.right, g.left)[message % 2]
        return pltpu.make_async_remote_copy(
            src, dst, self.send.at[q, message], self.recv.at[q, message], device_id={g.axis: to}
        )

    def first(self, q):
        for h in (0, 1):
            self.out1[q, h] = self.rows(q, self.group.at(2, h)).astype(BF16)
            self.copy(q, h).start()

    def second(self, q):
        g, sub = self.group, self.sub
        for side, step in ((0, 1), (1, 3)):
            self.copy(q, side).wait_recv()
            for h in (0, 1):
                value = self.rows(q, g.at(step, h))
                if h == side:
                    value = value + self.in1[q, side].astype(F32)
                self.out2[q, side, h * sub:(h + 1) * sub, :] = value.astype(BF16)
            self.copy(q, 2 + side).start()

    def third(self, q):
        g, sub = self.group, self.sub
        self.copy(q, 2).wait_recv()
        self.copy(q, 3).wait_recv()

        def total(h):
            rows = pl.ds(pl.multiple_of(h * sub, sub), sub)
            return (
                self.rows(q, g.at(0, h))
                + self.in2[q, 0, rows, :].astype(F32)
                + self.in2[q, 1, rows, :].astype(F32)
            )

        self.out3[q] = total(1 - g.half).astype(self.out3.dtype)
        self.copy(q, 4).start()
        self.keep[q] = total(g.half)

    def last(self, q):
        self.copy(q, 4).wait_recv()
        return self.keep[q] + self.in3[q].astype(F32)

    def drain(self, q):
        for message in range(5):
            self.copy(q, message).wait_send()


def product(a, a_other, w, w_other, sums, q, arrived):
    cols = sums.shape[2]
    tile = 256
    for part in range(cols // tile):
        at = slice(part * tile, (part + 1) * tile)
        sums[q % 4, :, at] = jnp.dot(a[q], w[:, at], preferred_element_type=F32)
    arrived()
    for part in range(cols // tile):
        at = slice(part * tile, (part + 1) * tile)
        sums[q % 4, :, at] += jnp.dot(a_other[q], w_other[:, at], preferred_element_type=F32)


def kernel(
    res, encw, decw, encb, decb, active,
    codes_out, rebuilt_out,
    x_own, x_sib, c_own, c_sib, we_own, we_sib, wd_own, wd_sib, mask, made,
    e_sums, e_out1, e_in1, e_out2, e_in2, e_out3, e_in3, e_keep,
    d_sums, d_out1, d_in1, d_out2, d_in2, d_out3, d_in3, d_keep,
    a2a_send, a2a_recv, local_sem, wx_sem,
    xg_send, xg_recv, cg_send, cg_recv,
    xs_send, xs_recv, cs_send, cs_recv,
    er_send, er_recv, dr_send, dr_recv, co_sem, ro_sem,
):
    tok, lat, core = Group("tok"), Group("lat"), lax.axis_index("src")
    t, l = tok.me, lat.me
    sibling = {"src": 1 - core}
    width = x_own.shape[2]
    sub = x_own.shape[1] // PARTS
    alone = t == l

    def half(which):
        return pl.ds(pl.multiple_of(which * width, width), width)

    def block(index):
        return pl.ds(pl.multiple_of(index * sub, sub), sub)

    loads = [
        pltpu.make_async_copy(encw.at[:, half(core)], we_own, local_sem.at[0]),
        pltpu.make_async_copy(decw.at[half(core), :], wd_own, local_sem.at[1]),
        pltpu.make_async_copy(decw.at[half(1 - core), :], wd_sib, local_sem.at[2]),
        pltpu.make_async_copy(active.at[:, half(core)], mask, local_sem.at[3]),
    ]
    for load in loads:
        load.start()

    barrier = pltpu.get_barrier_semaphore()
    for device in tok.neighbours() + lat.neighbours() + [sibling]:
        pl.semaphore_signal(barrier, inc=1, device_id=device)

    @pl.loop(0, PARTS)
    def _(i):
        @pl.when(jnp.logical_not(alone & (i == t)))
        def _():
            pl.semaphore_signal(barrier, inc=1, device_id={"tok": i, "lat": t})

    pl.semaphore_wait(barrier, jnp.where(alone, 14, 15))

    def relay(q):
        j = (t - q + PARTS) % PARTS
        return pltpu.make_async_remote_copy(
            res.at[block(j), :], x_own.at[q, block(j), :], a2a_send.at[q], a2a_recv.at[q],
            device_id={"tok": l, "lat": j},
        )

    def stay():
        return pltpu.make_async_copy(res.at[block(l), :], x_own.at[0, block(l), :], a2a_recv.at[0])

    @pl.loop(0, PARTS)
    def _(q):
        own = alone & (q == 0)

        @pl.when(own)
        def _():
            stay().start()

        @pl.when(jnp.logical_not(own))
        def _():
            relay(q).start()

    def landed(q):
        own = alone & (q == 0)
        place = x_own.at[q, block(l), :]

        @pl.when(own)
        def _():
            stay().wait()

        @pl.when(jnp.logical_not(own))
        def _():
            pltpu.make_async_remote_copy(
                place, place, a2a_send.at[q], a2a_recv.at[q], device_id=sibling
            ).wait_recv()

    swap = pltpu.make_async_remote_copy(
        encw.at[:, half(1 - core)], we_sib, wx_sem.at[0], wx_sem.at[1], device_id=sibling
    )
    swap.start()

    xg = Gather(lat, x_own, xg_send, xg_recv, sub)
    cg = Gather(tok, c_own, cg_send, cg_recv, sub)
    er = Scatter(
        tok, e_sums, lambda q, owner: (owner - q + PARTS) % PARTS,
        e_out1, e_in1, e_out2, e_in2, e_out3, e_in3, e_keep, er_send, er_recv, sub,
    )
    dr = Scatter(
        lat, d_sums, lambda q, owner: owner,
        d_out1, d_in1, d_out2, d_in2, d_out3, d_in3, d_keep, dr_send, dr_recv, sub,
    )

    def x_swap(q):
        return pltpu.make_async_remote_copy(
            x_own.at[q], x_sib.at[q], xs_send.at[q], xs_recv.at[q], device_id=sibling
        )

    def c_swap(q):
        return pltpu.make_async_remote_copy(
            c_own.at[q], c_sib.at[q], cs_send.at[q], cs_recv.at[q], device_id=sibling
        )

    def codes_copy(q, which):
        rows = block((t - q + PARTS) % PARTS)
        src = c_sib if which else c_own
        col = (1 - core) if which else core
        return pltpu.make_async_copy(
            src.at[q, block(t), :], codes_out.at[rows, half(col)], co_sem.at[q, which]
        )

    def rebuilt_copy(q):
        rows = block((l - q + PARTS) % PARTS)
        return pltpu.make_async_copy(made.at[q], rebuilt_out.at[rows, :], ro_sem.at[q])

    def s0(q):
        landed(q)
        xg.first(q)

    def s3(q):
        xg.last(q)
        x_swap(q).start()

        @pl.when(q == 0)
        def _():
            loads[0].wait()
            swap.wait()

        product(x_own, x_sib, we_own, we_sib, e_sums, q, lambda: x_swap(q).wait_recv())
        er.first(q)

    def s6(q):
        @pl.when(q == 0)
        def _():
            loads[3].wait()

        value = er.last(q) + encb[pl.ds(core, 1), :]
        kept = mask[block((t - q + PARTS) % PARTS), :] == 1
        c_own[q, block(t), :] = jnp.where(kept, jnp.maximum(value, 0.0), 0.0).astype(BF16)
        cg.first(q)
        codes_copy(q, 0).start()

    def s9(q):
        cg.last(q)
        c_swap(q).start()

        @pl.when(q == 0)
        def _():
            loads[1].wait()
            loads[2].wait()

        product(c_own, c_sib, wd_own, wd_sib, d_sums, q, lambda: c_swap(q).wait_recv())
        dr.first(q)
        codes_copy(q, 1).start()

    def s12(q):
        made[q] = (dr.last(q) + decb[...]).astype(BF16)
        rebuilt_copy(q).start()

    stages = [
        s0, xg.second, xg.third, s3, er.second, er.third, s6,
        cg.second, cg.third, s9, dr.second, dr.third, s12,
    ]

    @pl.loop(0, PARTS + len(stages) - 1)
    def _(i):
        for number, stage in reversed(list(enumerate(stages))):
            q = i - number

            @pl.when((q >= 0) & (q < PARTS))
            def _(stage=stage, q=q):
                stage(q)

    @pl.loop(0, PARTS)
    def _(q):
        @pl.when(jnp.logical_not(alone & (q == 0)))
        def _():
            relay(q).wait_send()

        xg.drain(q)
        cg.drain(q)
        er.drain(q)
        dr.drain(q)
        x_swap(q).wait_send()
        c_swap(q).wait_send()
        codes_copy(q, 0).wait()
        codes_copy(q, 1).wait()
        rebuilt_copy(q).wait()


def per_device(residuals, enc_weight, dec_weight, enc_bias, dec_bias, active):
    rows, width = residuals.shape[1:]
    latents = enc_weight.shape[2]
    sub = rows // PARTS
    dma = pltpu.SemaphoreType.DMA

    def reduction():
        return [
            pltpu.VMEM((4, rows, width), F32),
            pltpu.VMEM((PARTS, 2, sub, width), BF16),
            pltpu.VMEM((PARTS, 2, sub, width), BF16),
            pltpu.VMEM((PARTS, 2, 2 * sub, width), BF16),
            pltpu.VMEM((PARTS, 2, 2 * sub, width), BF16),
            pltpu.VMEM((PARTS, sub, width), BF16),
            pltpu.VMEM((PARTS, sub, width), BF16),
            pltpu.VMEM((PARTS, sub, width), F32),
        ]

    anywhere = pl.BlockSpec(memory_space=pl.ANY)
    vmem = pl.BlockSpec(memory_space=pltpu.VMEM)
    codes, rebuilt = pl.pallas_call(
        kernel,
        out_shape=(
            jax.ShapeDtypeStruct((rows, latents), BF16),
            jax.ShapeDtypeStruct((rows, width), BF16),
        ),
        in_specs=[anywhere, anywhere, anywhere, vmem, vmem, anywhere],
        out_specs=(anywhere, anywhere),
        scratch_shapes=[pltpu.VMEM((PARTS, rows, width), BF16)] * 4
        + [pltpu.VMEM((width, width), BF16)] * 4
        + [pltpu.VMEM((rows, width), jnp.int32), pltpu.VMEM((PARTS, sub, width), BF16)]
        + reduction()
        + reduction()
        + [dma((PARTS,)), dma((PARTS,)), dma((4,)), dma((2,))]
        + [dma((PARTS, 7))] * 4
        + [dma((PARTS,))] * 4
        + [dma((PARTS, 5))] * 4
        + [dma((PARTS, 2)), dma((PARTS,))],
        compiler_params=pltpu.CompilerParams(
            collective_id=0, has_side_effects=True, vmem_limit_bytes=60 * 1024 * 1024
        ),
    )(
        residuals[0], enc_weight[0], dec_weight[0],
        enc_bias.reshape(2, width), dec_bias, active,
    )
    return codes, rebuilt[None]


def solution(mesh):
    return jax.shard_map(
        per_device,
        mesh=mesh,
        in_specs=(
            P("src", "tok", "lat"),
            P("src", "tok", "lat"),
            P("src", "lat", "tok"),
            P("lat"),
            P("src", "tok"),
            P("tok", "lat"),
        ),
        out_specs=(P("tok", "lat"), P("src", "lat", "tok")),
        check_vma=False,
    )
```

```python
import jax
import jax.numpy as jnp
from jax import lax
from jax.experimental import pallas as pl
from jax.experimental.pallas import tpu as pltpu
from jax.sharding import PartitionSpec as P

PARTS = 8
SLOTS = 6
RING = 4
BF16 = jnp.bfloat16
F32 = jnp.float32


class Group:
    def __init__(self, axis):
        self.axis = axis
        self.me = lax.axis_index(axis)
        self.ring = self.me // 2
        self.half = self.me % 2
        self.right = self.at(1, self.half)
        self.left = self.at(3, self.half)
        self.partner = self.at(0, 1 - self.half)

    def at(self, step, half):
        return 2 * ((self.ring + step) % RING) + half

    def neighbours(self):
        return [{self.axis: self.right}, {self.axis: self.left}, {self.axis: self.partner}]


class Gather:
    def __init__(self, group, buf, send, recv, sub):
        self.group, self.buf, self.send, self.recv, self.sub = group, buf, send, recv, sub

    def copy(self, q, block, message, to):
        rows = pl.ds(pl.multiple_of(block * self.sub, self.sub), self.sub)
        place = self.buf.at[q, rows, :]
        return pltpu.make_async_remote_copy(
            place, place, self.send.at[0], self.recv.at[q, (1, 0, 3, 3, 2, 3, 3)[message]],
            device_id={self.group.axis: to},
        )

    def first(self, q):
        g = self.group
        self.copy(q, g.me, 1, g.right).start()
        self.copy(q, g.me, 2, g.left).start()
        self.copy(q, g.me, 0, g.partner).start()

    def pass_left(self, q):
        g = self.group
        self.copy(q, g.left, 1, g.right).wait_recv()
        self.copy(q, g.left, 5, g.right).start()

    def pass_partner(self, q):
        g = self.group
        self.copy(q, g.partner, 0, g.partner).wait_recv()
        self.copy(q, g.partner, 4, g.left).start()
        self.copy(q, g.partner, 3, g.right).start()

    def pass_corner(self, q):
        g = self.group
        self.copy(q, g.at(1, 1 - g.half), 4, g.right).wait_recv()
        self.copy(q, g.at(1, 1 - g.half), 6, g.left).start()

    def last(self, q):
        rest = self.buf.at[q, pl.ds(0, 4 * self.sub), :]
        pltpu.make_async_remote_copy(
            rest, rest, self.send.at[0], self.recv.at[q, 3], device_id={self.group.axis: self.group.right}
        ).wait_recv()


class Scatter:
    def __init__(self, group, sums, place, out1, in1, out2, in2, out3, in3, keep, send, recv, sub):
        self.group, self.sums, self.place = group, sums, place
        self.out1, self.in1, self.out2, self.in2 = out1, in1, out2, in2
        self.out3, self.in3, self.keep = out3, in3, keep
        self.send, self.recv, self.sub = send, recv, sub

    def rows(self, q, owner):
        start = pl.multiple_of(self.place(q, owner) * self.sub, self.sub)
        return self.sums[q % SLOTS, pl.ds(start, self.sub), :]

    def copy(self, q, message):
        g = self.group
        src, dst = {
            0: (self.out1.at[q, 0], self.in1.at[q, 0]),
            1: (self.out1.at[q, 1], self.in1.at[q, 1]),
            2: (self.out2.at[q, 0], self.in2.at[q, 0]),
            3: (self.out2.at[q, 1], self.in2.at[q, 1]),
            4: (self.out3.at[q], self.in3.at[q]),
        }[message]
        to = g.partner if message == 4 else (g.right, g.left)[message % 2]
        return pltpu.make_async_remote_copy(
            src, dst, self.send.at[0], self.recv.at[q, (0, 1, 2, 2, 3)[message]], device_id={g.axis: to}
        )

    def first(self, q):
        for h in (0, 1):
            self.out1[q, h] = self.rows(q, self.group.at(2, h)).astype(BF16)
            self.copy(q, h).start()

    def second(self, q):
        g, sub = self.group, self.sub
        for side, step in ((0, 1), (1, 3)):
            self.copy(q, side).wait_recv()
            for h in (0, 1):
                value = self.rows(q, g.at(step, h))
                if h == side:
                    value = value + self.in1[q, side].astype(F32)
                self.out2[q, side, h * sub:(h + 1) * sub, :] = value.astype(BF16)
            self.copy(q, 2 + side).start()

    def third(self, q):
        g, sub = self.group, self.sub
        pltpu.make_async_remote_copy(
            self.out2.at[q], self.in2.at[q], self.send.at[0], self.recv.at[q, 2], device_id={g.axis: g.right}
        ).wait_recv()

        def total(h):
            rows = pl.ds(pl.multiple_of(h * sub, sub), sub)
            return (
                self.rows(q, g.at(0, h))
                + self.in2[q, 0, rows, :].astype(F32)
                + self.in2[q, 1, rows, :].astype(F32)
            )

        self.out3[q] = total(1 - g.half).astype(self.out3.dtype)
        self.copy(q, 4).start()
        self.keep[q] = total(g.half)

    def last(self, q):
        self.copy(q, 4).wait_recv()
        return self.keep[q] + self.in3[q].astype(F32)


def product(a, a_other, w, w_other, sums, q, arrived):
    cols = sums.shape[2]
    tile = 256
    for part in range(cols // tile):
        at = slice(part * tile, (part + 1) * tile)
        sums[q % SLOTS, :, at] = jnp.dot(a[q], w[:, at], preferred_element_type=F32)
    arrived()
    for part in range(cols // tile):
        at = slice(part * tile, (part + 1) * tile)
        sums[q % SLOTS, :, at] += jnp.dot(a_other[q], w_other[:, at], preferred_element_type=F32)


def kernel(
    res, encw, decw, encb, decb, active,
    codes_out, rebuilt_out,
    x_own, x_sib, c_own, c_sib, we_own, we_sib, wd_own, wd_sib, mask, made,
    e_sums, e_out1, e_in1, e_out2, e_in2, e_out3, e_in3, e_keep,
    d_sums, d_out1, d_in1, d_out2, d_in2, d_out3, d_in3, d_keep,
    a2a_send, a2a_recv, local_sem, wx_sem,
    xg_send, xg_recv, cg_send, cg_recv,
    xs_send, xs_recv, cs_send, cs_recv,
    er_send, er_recv, dr_send, dr_recv, co_sem, ro_sem,
):
    tok, lat, core = Group("tok"), Group("lat"), lax.axis_index("src")
    t, l = tok.me, lat.me
    sibling = {"src": 1 - core}
    width = x_own.shape[2]
    sub = x_own.shape[1] // PARTS
    alone = t == l

    def half(which):
        return pl.ds(pl.multiple_of(which * width, width), width)

    def block(index):
        return pl.ds(pl.multiple_of(index * sub, sub), sub)

    loads = [
        pltpu.make_async_copy(encw.at[:, half(core)], we_own, local_sem.at[0]),
        pltpu.make_async_copy(decw.at[half(core), :], wd_own, local_sem.at[1]),
        pltpu.make_async_copy(decw.at[half(1 - core), :], wd_sib, local_sem.at[2]),
        pltpu.make_async_copy(active.at[:, half(core)], mask, local_sem.at[3]),
    ]
    for load in loads:
        load.start()

    barrier = pltpu.get_barrier_semaphore()
    for device in tok.neighbours() + lat.neighbours() + [sibling]:
        pl.semaphore_signal(barrier, inc=1, device_id=device)

    @pl.loop(0, PARTS)
    def _(i):
        @pl.when(jnp.logical_not(alone & (i == t)))
        def _():
            pl.semaphore_signal(barrier, inc=1, device_id={"tok": i, "lat": t})

    pl.semaphore_wait(barrier, jnp.where(alone, 14, 15))

    def relay(q):
        j = (t - q + PARTS) % PARTS
        return pltpu.make_async_remote_copy(
            res.at[block(j), :], x_own.at[q, block(j), :], a2a_send.at[0], a2a_recv.at[q],
            device_id={"tok": l, "lat": j},
        )

    def stay():
        return pltpu.make_async_copy(res.at[block(l), :], x_own.at[0, block(l), :], a2a_recv.at[0])

    @pl.loop(0, PARTS)
    def _(q):
        own = alone & (q == 0)

        @pl.when(own)
        def _():
            stay().start()

        @pl.when(jnp.logical_not(own))
        def _():
            relay(q).start()

    def landed(q):
        own = alone & (q == 0)
        place = x_own.at[q, block(l), :]

        @pl.when(own)
        def _():
            stay().wait()

        @pl.when(jnp.logical_not(own))
        def _():
            pltpu.make_async_remote_copy(
                place, place, a2a_send.at[0], a2a_recv.at[q], device_id=sibling
            ).wait_recv()

    swap = pltpu.make_async_remote_copy(
        encw.at[:, half(1 - core)], we_sib, wx_sem.at[0], wx_sem.at[1], device_id=sibling
    )
    swap.start()

    xg = Gather(lat, x_own, xg_send, xg_recv, sub)
    cg = Gather(tok, c_own, cg_send, cg_recv, sub)
    er = Scatter(
        tok, e_sums, lambda q, owner: (owner - q + PARTS) % PARTS,
        e_out1, e_in1, e_out2, e_in2, e_out3, e_in3, e_keep, er_send, er_recv, sub,
    )
    dr = Scatter(
        lat, d_sums, lambda q, owner: owner,
        d_out1, d_in1, d_out2, d_in2, d_out3, d_in3, d_keep, dr_send, dr_recv, sub,
    )

    def x_swap(q):
        return pltpu.make_async_remote_copy(
            x_own.at[q], x_sib.at[q], xs_send.at[0], xs_recv.at[q], device_id=sibling
        )

    def c_swap(q):
        return pltpu.make_async_remote_copy(
            c_own.at[q], c_sib.at[q], cs_send.at[0], cs_recv.at[q], device_id=sibling
        )

    def codes_copy(q, which):
        rows = block((t - q + PARTS) % PARTS)
        src = c_sib if which else c_own
        col = (1 - core) if which else core
        return pltpu.make_async_copy(
            src.at[q, block(t), :], codes_out.at[rows, half(col)], co_sem.at[0]
        )

    def rebuilt_copy(q):
        rows = block((l - q + PARTS) % PARTS)
        return pltpu.make_async_copy(made.at[q], rebuilt_out.at[rows, :], ro_sem.at[0])

    def x_first(q):
        landed(q)
        xg.first(q)

    def x_last(q):
        xg.last(q)
        x_swap(q).start()

    def encode(q):
        @pl.when(q == 0)
        def _():
            loads[0].wait()
            swap.wait_recv()

        product(x_own, x_sib, we_own, we_sib, e_sums, q, lambda: x_swap(q).wait_recv())
        er.first(q)

    def activate(q):
        @pl.when(q == 0)
        def _():
            loads[3].wait()

        value = er.last(q) + encb[:, half(core)]
        kept = mask[block((t - q + PARTS) % PARTS), :] == 1
        c_own[q, block(t), :] = jnp.where(kept, jnp.maximum(value, 0.0), 0.0).astype(BF16)
        cg.first(q)
        codes_copy(q, 0).start()

    def c_last(q):
        cg.last(q)
        c_swap(q).start()

    def decode(q):
        @pl.when(q == 0)
        def _():
            loads[1].wait()
            loads[2].wait()

        product(c_own, c_sib, wd_own, wd_sib, d_sums, q, lambda: c_swap(q).wait_recv())
        dr.first(q)
        codes_copy(q, 1).start()

    def finish(q):
        made[q] = (dr.last(q) + decb[...]).astype(BF16)
        rebuilt_copy(q).start()

    steps = [
        (encode, 5),
        (dr.third, 17),
        (dr.second, 13),
        (cg.pass_corner, 10),
        (cg.pass_partner, 9),
        (er.second, 6),
        (x_last, 4),
        (xg.pass_corner, 3),
        (xg.pass_left, 2),
        (x_first, 0),
        (xg.pass_partner, 1),
        (activate, 8),
        (er.third, 7),
        (decode, 11),
        (finish, 19),
        (cg.pass_left, 9),
        (c_last, 10),
    ]
    rounds = PARTS + max(lag for _, lag in steps)

    @pl.loop(0, rounds)
    def _(i):
        for step, lag in steps:
            q = i - lag

            @pl.when((q >= 0) & (q < PARTS))
            def _(step=step, q=q):
                step(q)

    def sent(src, sem):
        pltpu.make_async_remote_copy(src, src, sem, a2a_recv.at[0], device_id=sibling).wait_send()

    most = pl.ds(0, PARTS - 1)
    for sem in (xg_send, cg_send, er_send, dr_send):
        sent(x_own.at[most], sem.at[0])
    sent(x_own, xs_send.at[0])
    sent(c_own, cs_send.at[0])
    swap.wait_send()

    @pl.when(alone)
    def _():
        sent(res.at[pl.ds(0, (PARTS - 1) * sub), :], a2a_send.at[0])

    @pl.when(jnp.logical_not(alone))
    def _():
        sent(res, a2a_send.at[0])

    pltpu.make_async_copy(codes_out, codes_out, co_sem.at[0]).wait()
    pltpu.make_async_copy(rebuilt_out, rebuilt_out, ro_sem.at[0]).wait()


def deliver(codes_in, rebuilt_in, codes_out, rebuilt_out):
    codes_out[...] = codes_in[...]
    rebuilt_out[...] = rebuilt_in[...]


def per_device(residuals, enc_weight, dec_weight, enc_bias, dec_bias, active):
    rows, width = residuals.shape[1:]
    latents = enc_weight.shape[2]
    sub = rows // PARTS
    dma = pltpu.SemaphoreType.DMA

    def reduction():
        return [
            pltpu.VMEM((SLOTS, rows, width), F32),
            pltpu.VMEM((PARTS, 2, sub, width), BF16),
            pltpu.VMEM((PARTS, 2, sub, width), BF16),
            pltpu.VMEM((PARTS, 2, 2 * sub, width), BF16),
            pltpu.VMEM((PARTS, 2, 2 * sub, width), BF16),
            pltpu.VMEM((PARTS, sub, width), BF16),
            pltpu.VMEM((PARTS, sub, width), BF16),
            pltpu.VMEM((PARTS, sub, width), F32),
        ]

    anywhere = pl.BlockSpec(memory_space=pl.ANY)
    vmem = pl.BlockSpec(memory_space=pltpu.VMEM)
    codes, rebuilt = pl.pallas_call(
        kernel,
        out_shape=(
            jax.ShapeDtypeStruct((rows, latents), BF16),
            jax.ShapeDtypeStruct((rows, width), BF16),
        ),
        in_specs=[anywhere, anywhere, anywhere, vmem, vmem, anywhere],
        out_specs=(anywhere, anywhere),
        scratch_shapes=[pltpu.VMEM((PARTS, rows, width), BF16)] * 4
        + [pltpu.VMEM((width, width), BF16)] * 4
        + [pltpu.VMEM((rows, width), jnp.int32), pltpu.VMEM((PARTS, sub, width), BF16)]
        + reduction()
        + reduction()
        + [dma((1,)), dma((PARTS,)), dma((4,)), dma((2,))]
        + [dma((1,)), dma((PARTS, 4))] * 2
        + [dma((1,)), dma((PARTS,))] * 2
        + [dma((1,)), dma((PARTS, 4))] * 2
        + [dma((1,)), dma((1,))],
        compiler_params=pltpu.CompilerParams(
            collective_id=0, has_side_effects=True, vmem_limit_bytes=60 * 1024 * 1024
        ),
    )(
        residuals[0], enc_weight[0], dec_weight[0],
        enc_bias.reshape(1, latents), dec_bias, active,
    )
    codes, rebuilt = pl.pallas_call(
        deliver,
        out_shape=(
            jax.ShapeDtypeStruct(codes.shape, BF16),
            jax.ShapeDtypeStruct(rebuilt.shape, BF16),
        ),
        grid=(2,),
        in_specs=[pl.BlockSpec((rows // 2, latents), lambda i: (i, 0)), pl.BlockSpec((rows // 2, width), lambda i: (i, 0))],
        out_specs=(pl.BlockSpec((rows // 2, latents), lambda i: (i, 0)), pl.BlockSpec((rows // 2, width), lambda i: (i, 0))),
    )(codes, rebuilt)
    return codes, rebuilt[None]


def solution(mesh):
    return jax.shard_map(
        per_device,
        mesh=mesh,
        in_specs=(
            P("src", "tok", "lat"),
            P("src", "tok", "lat"),
            P("src", "lat", "tok"),
            P("lat"),
            P("src", "tok"),
            P("tok", "lat"),
        ),
        out_specs=(P("tok", "lat"), P("src", "lat", "tok")),
        check_vma=False,
    )
```

```python
import jax
import jax.numpy as jnp
from jax import lax
from jax.experimental import pallas as pl
from jax.experimental.pallas import tpu as pltpu
from jax.sharding import PartitionSpec as P

PARTS = 8
SLOTS = 6
PAIR_FIRST = (5, 6, 7)
LAT_FIRST = ()
PAIR_LAST = ()
RING = 4
BF16 = jnp.bfloat16
F32 = jnp.float32


class Group:
    def __init__(self, axis):
        self.axis = axis
        self.me = lax.axis_index(axis)
        self.ring = self.me // 2
        self.half = self.me % 2
        self.right = self.at(1, self.half)
        self.left = self.at(3, self.half)
        self.partner = self.at(0, 1 - self.half)

    def at(self, step, half):
        return 2 * ((self.ring + step) % RING) + half

    def neighbours(self):
        return [{self.axis: self.right}, {self.axis: self.left}, {self.axis: self.partner}]


def either(q, chunks, special, usual):
    if not chunks:
        usual(q)
        return
    named = q == chunks[0]
    for chunk in chunks[1:]:
        named = named | (q == chunk)

    @pl.when(named)
    def _():
        special(q)

    @pl.when(jnp.logical_not(named))
    def _():
        usual(q)


class Gather:
    def __init__(self, group, buf, send, recv, sub, pair_last=()):
        self.group, self.buf, self.send, self.recv, self.sub = group, buf, send, recv, sub
        self.pair_last = pair_last

    def copy(self, q, block, sem, to, skip=0, rows=None):
        rows = rows or self.sub
        start = pl.multiple_of(block * self.sub + skip, rows)
        place = self.buf.at[q, pl.ds(start, rows), :]
        return pltpu.make_async_remote_copy(
            place, place, self.send.at[0], self.recv.at[q, sem], device_id={self.group.axis: to}
        )

    def first(self, q):
        g = self.group
        self.copy(q, g.me, 0, g.right).start()
        either(
            q, self.pair_last,
            lambda q: self.copy(q, g.me, 1, g.left).start(),
            lambda q: self.copy(q, g.me, 3, g.left).start(),
        )
        either(
            q, self.pair_last,
            lambda q: self.copy(q, g.me, 3, g.partner).start(),
            lambda q: self.copy(q, g.me, 1, g.partner).start(),
        )

    def pass_left(self, q):
        g = self.group
        self.copy(q, g.left, 0, g.right).wait_recv()

        def special(q):
            self.copy(q, g.left, 2, g.right, 0, self.sub // 2).start()
            self.copy(q, g.left, 3, g.partner).start()

        either(q, self.pair_last, special, lambda q: self.copy(q, g.left, 3, g.right).start())

    def pass_other(self, q):
        g = self.group

        def special(q):
            self.copy(q, g.right, 1, g.left).wait_recv()
            self.copy(q, g.right, 2, g.left, self.sub // 2, self.sub // 2).start()
            self.copy(q, g.right, 3, g.partner).start()

        def usual(q):
            self.copy(q, g.partner, 1, g.partner).wait_recv()
            self.copy(q, g.partner, 2, g.left).start()
            self.copy(q, g.partner, 3, g.right).start()

        either(q, self.pair_last, special, usual)

    def pass_far(self, q):
        g = self.group

        def special(q):
            self.copy(q, g.at(2, g.half), 2, g.right).wait_recv()
            self.copy(q, g.at(2, g.half), 3, g.partner).start()

        def usual(q):
            self.copy(q, g.at(1, 1 - g.half), 2, g.right).wait_recv()
            self.copy(q, g.at(1, 1 - g.half), 3, g.left).start()

        either(q, self.pair_last, special, usual)

    def last(self, q):
        rest = self.buf.at[q, pl.ds(0, 4 * self.sub), :]
        pltpu.make_async_remote_copy(
            rest, rest, self.send.at[0], self.recv.at[q, 3], device_id={self.group.axis: self.group.right}
        ).wait_recv()


class Scatter:
    def __init__(self, group, sums, place, out1, in1, out2, in2, out3, in3, out4, in4, keep, send, recv, sub, pair_first=()):
        self.group, self.sums, self.place = group, sums, place
        self.out1, self.in1, self.out2, self.in2 = out1, in1, out2, in2
        self.out3, self.in3, self.out4, self.in4, self.keep = out3, in3, out4, in4, keep
        self.send, self.recv, self.sub, self.pair_first = send, recv, sub, pair_first

    def rows(self, q, owner):
        start = pl.multiple_of(self.place(q, owner) * self.sub, self.sub)
        return (q % SLOTS, pl.ds(start, self.sub), slice(None))

    def copy(self, q, src, dst, sem, to):
        return pltpu.make_async_remote_copy(
            src, dst, self.send.at[0], self.recv.at[q, sem], device_id={self.group.axis: to}
        )

    def side(self, q, side):
        to = (self.group.right, self.group.left)[side]
        return self.copy(q, self.out1.at[q, side], self.in1.at[q, side], side, to)

    def near(self, q, side):
        to = (self.group.right, self.group.left)[side]
        rows = pl.ds(0, self.sub // 2)
        return self.copy(q, self.out1.at[q, side, rows, :], self.in1.at[q, side, rows, :], side, to)

    def double(self, q):
        return self.copy(q, self.out2.at[q], self.in2.at[q], 2, self.group.partner)

    def single(self, q):
        return self.copy(q, self.out3.at[q], self.in3.at[q], 3, self.group.partner)

    def first(self, q):
        g, sub = self.group, self.sub

        def special(q):
            for step in range(RING):
                at = slice((step % 2) * sub, (step % 2 + 1) * sub)
                self.out2[q, step // 2, at, :] = self.sums[self.rows(q, g.at(step, 1 - g.half))].astype(BF16)
            self.double(q).start()

        def usual(q):
            for h in (0, 1):
                self.out1[q, h] = self.sums[self.rows(q, g.at(2, h))].astype(BF16)
                self.side(q, h).start()

        either(q, self.pair_first, special, usual)

    def second(self, q):
        g, sub = self.group, self.sub

        def special(q):
            self.double(q).wait_recv()
            for step in (2, 1, 3, 0):
                at = slice((step % 2) * sub, (step % 2 + 1) * sub)
                value = self.sums[self.rows(q, g.at(step, g.half))] + self.in2[q, step // 2, at, :].astype(F32)
                if step == 2:
                    for side in (0, 1):
                        part = slice(side * sub // 2, (side + 1) * sub // 2)
                        self.out1[q, side, 0:sub // 2, :] = value[part].astype(BF16)
                        self.near(q, side).start()
                elif step == 0:
                    self.keep[q] = value
                else:
                    self.sums[self.rows(q, g.at(step, g.half))] = value

        def usual(q):
            for side, step in ((0, 1), (1, 3)):
                self.side(q, side).wait_recv()
                for h in (0, 1):
                    value = self.sums[self.rows(q, g.at(step, h))]
                    if h == side:
                        value = value + self.in1[q, side].astype(F32)
                    self.out2[q, side, h * sub:(h + 1) * sub, :] = value.astype(BF16)
                to = (g.right, g.left)[side]
                self.copy(q, self.out2.at[q, side], self.in2.at[q, side], 2, to).start()

        either(q, self.pair_first, special, usual)

    def third(self, q):
        g, sub = self.group, self.sub

        def special(q):
            for side, step in ((0, 1), (1, 3)):
                self.near(q, side).wait_recv()
                value = self.sums[self.rows(q, g.at(step, g.half))]
                part = slice(side * sub // 2, (side + 1) * sub // 2)
                rest = slice((1 - side) * sub // 2, (2 - side) * sub // 2)
                relayed = value[part] + self.in1[q, side, 0:sub // 2, :].astype(F32)
                self.out4[q, side, part, :] = relayed.astype(BF16)
                self.out4[q, side, rest, :] = value[rest].astype(BF16)
                to = (g.right, g.left)[side]
                self.copy(q, self.out4.at[q, side], self.in4.at[q, side], 3, to).start()

        def usual(q):
            self.copy(q, self.out2.at[q], self.in2.at[q], 2, g.right).wait_recv()

            def total(h):
                rows = pl.ds(pl.multiple_of(h * sub, sub), sub)
                return (
                    self.sums[self.rows(q, g.at(0, h))]
                    + self.in2[q, 0, rows, :].astype(F32)
                    + self.in2[q, 1, rows, :].astype(F32)
                )

            self.out3[q] = total(1 - g.half).astype(BF16)
            self.single(q).start()
            self.keep[q] = total(g.half)

        either(q, self.pair_first, special, usual)

    def last(self, q):
        def special(q):
            self.copy(q, self.out4.at[q], self.in4.at[q], 3, self.group.right).wait_recv()
            self.keep[q] += self.in4[q, 0].astype(F32) + self.in4[q, 1].astype(F32)

        def usual(q):
            self.single(q).wait_recv()
            self.keep[q] += self.in3[q].astype(F32)

        either(q, self.pair_first, special, usual)
        return self.keep[q]


def product(a, a_other, w, w_other, sums, q, arrived):
    cols = sums.shape[2]
    tile = 256
    for part in range(cols // tile):
        at = slice(part * tile, (part + 1) * tile)
        sums[q % SLOTS, :, at] = jnp.dot(a[q], w[:, at], preferred_element_type=F32)
    arrived()
    for part in range(cols // tile):
        at = slice(part * tile, (part + 1) * tile)
        sums[q % SLOTS, :, at] += jnp.dot(a_other[q], w_other[:, at], preferred_element_type=F32)


def kernel(
    res, encw, decw, encb, decb, active,
    codes_out, rebuilt_out,
    x_own, x_sib, c_own, c_sib, we_own, we_sib, wd_own, wd_sib, mask, made,
    e_sums, e_out1, e_in1, e_out2, e_in2, e_out3, e_in3, e_out4, e_in4, e_keep,
    d_sums, d_out1, d_in1, d_out2, d_in2, d_out3, d_in3, d_out4, d_in4, d_keep,
    a2a_send, a2a_recv, local_sem, wx_sem,
    xg_send, xg_recv, cg_send, cg_recv,
    xs_send, xs_recv, cs_send, cs_recv,
    er_send, er_recv, dr_send, dr_recv, co_sem, ro_sem,
):
    tok, lat, core = Group("tok"), Group("lat"), lax.axis_index("src")
    t, l = tok.me, lat.me
    sibling = {"src": 1 - core}
    width = x_own.shape[2]
    sub = x_own.shape[1] // PARTS
    alone = t == l

    def half(which):
        return pl.ds(pl.multiple_of(which * width, width), width)

    def block(index):
        return pl.ds(pl.multiple_of(index * sub, sub), sub)

    loads = [
        pltpu.make_async_copy(encw.at[:, half(core)], we_own, local_sem.at[0]),
        pltpu.make_async_copy(decw.at[half(core), :], wd_own, local_sem.at[1]),
        pltpu.make_async_copy(decw.at[half(1 - core), :], wd_sib, local_sem.at[2]),
        pltpu.make_async_copy(active.at[:, half(core)], mask, local_sem.at[3]),
    ]
    for load in loads:
        load.start()

    barrier = pltpu.get_barrier_semaphore()
    for device in tok.neighbours() + lat.neighbours() + [sibling]:
        pl.semaphore_signal(barrier, inc=1, device_id=device)

    @pl.loop(0, PARTS)
    def _(i):
        @pl.when(jnp.logical_not(alone & (i == t)))
        def _():
            pl.semaphore_signal(barrier, inc=1, device_id={"tok": i, "lat": t})

    pl.semaphore_wait(barrier, jnp.where(alone, 14, 15))

    def relay(q):
        j = (t - q + PARTS) % PARTS
        return pltpu.make_async_remote_copy(
            res.at[block(j), :], x_own.at[q, block(j), :], a2a_send.at[0], a2a_recv.at[q],
            device_id={"tok": l, "lat": j},
        )

    def stay():
        return pltpu.make_async_copy(res.at[block(l), :], x_own.at[0, block(l), :], a2a_recv.at[0])

    @pl.loop(0, PARTS)
    def _(q):
        own = alone & (q == 0)

        @pl.when(own)
        def _():
            stay().start()

        @pl.when(jnp.logical_not(own))
        def _():
            relay(q).start()

    def landed(q):
        own = alone & (q == 0)
        place = x_own.at[q, block(l), :]

        @pl.when(own)
        def _():
            stay().wait()

        @pl.when(jnp.logical_not(own))
        def _():
            pltpu.make_async_remote_copy(
                place, place, a2a_send.at[0], a2a_recv.at[q], device_id=sibling
            ).wait_recv()

    swap = pltpu.make_async_remote_copy(
        encw.at[:, half(1 - core)], we_sib, wx_sem.at[0], wx_sem.at[1], device_id=sibling
    )
    swap.start()

    xg = Gather(lat, x_own, xg_send, xg_recv, sub)
    cg = Gather(tok, c_own, cg_send, cg_recv, sub, PAIR_LAST)
    er = Scatter(
        tok, e_sums, lambda q, owner: (owner - q + PARTS) % PARTS,
        e_out1, e_in1, e_out2, e_in2, e_out3, e_in3, e_out4, e_in4, e_keep, er_send, er_recv, sub, PAIR_FIRST,
    )
    dr = Scatter(
        lat, d_sums, lambda q, owner: owner,
        d_out1, d_in1, d_out2, d_in2, d_out3, d_in3, d_out4, d_in4, d_keep, dr_send, dr_recv, sub, LAT_FIRST,
    )

    def x_swap(q):
        return pltpu.make_async_remote_copy(
            x_own.at[q], x_sib.at[q], xs_send.at[0], xs_recv.at[q], device_id=sibling
        )

    def c_swap(q):
        return pltpu.make_async_remote_copy(
            c_own.at[q], c_sib.at[q], cs_send.at[0], cs_recv.at[q], device_id=sibling
        )

    def codes_copy(q, which):
        rows = block((t - q + PARTS) % PARTS)
        src = c_sib if which else c_own
        col = (1 - core) if which else core
        return pltpu.make_async_copy(
            src.at[q, block(t), :], codes_out.at[rows, half(col)], co_sem.at[0]
        )

    def rebuilt_copy(q):
        rows = block((l - q + PARTS) % PARTS)
        return pltpu.make_async_copy(made.at[q], rebuilt_out.at[rows, :], ro_sem.at[0])

    def x_first(q):
        landed(q)
        xg.first(q)

    def x_last(q):
        xg.last(q)
        x_swap(q).start()

    def encode(q):
        @pl.when(q == 0)
        def _():
            loads[0].wait()
            swap.wait_recv()

        product(x_own, x_sib, we_own, we_sib, e_sums, q, lambda: x_swap(q).wait_recv())
        er.first(q)

    def activate(q):
        @pl.when(q == 0)
        def _():
            loads[3].wait()

        value = er.last(q) + encb[:, half(core)]
        kept = mask[block((t - q + PARTS) % PARTS), :] == 1
        c_own[q, block(t), :] = jnp.where(kept, jnp.maximum(value, 0.0), 0.0).astype(BF16)
        cg.first(q)
        codes_copy(q, 0).start()

    def c_last(q):
        cg.last(q)
        c_swap(q).start()

    def decode(q):
        @pl.when(q == 0)
        def _():
            loads[1].wait()
            loads[2].wait()

        product(c_own, c_sib, wd_own, wd_sib, d_sums, q, lambda: c_swap(q).wait_recv())
        dr.first(q)
        codes_copy(q, 1).start()

    def finish(q):
        made[q] = (dr.last(q) + decb[...]).astype(BF16)
        rebuilt_copy(q).start()

    steps = [
        (c_last, 12),
        (dr.second, 14),
        (cg.pass_left, 10),
        (decode, 12),
        (er.second, 6),
        (er.third, 7),
        (cg.pass_other, 9),
        (cg.pass_far, 10),
        (activate, 8),
        (encode, 4),
        (xg.pass_left, 2),
        (xg.pass_other, 1),
        (finish, 17),
        (xg.pass_far, 2),
        (x_first, 0),
        (dr.third, 15),
        (x_last, 3),
    ]
    rounds = PARTS + max(lag for _, lag in steps)

    @pl.loop(0, rounds)
    def _(i):
        for step, lag in steps:
            q = i - lag

            @pl.when((q >= 0) & (q < PARTS))
            def _(step=step, q=q):
                step(q)

    def sent(src, sem):
        pltpu.make_async_remote_copy(src, src, sem, a2a_recv.at[0], device_id=sibling).wait_send()

    most = pl.ds(0, PARTS - 1)
    for sem in (xg_send, cg_send, er_send, dr_send):
        sent(x_own.at[most], sem.at[0])
    sent(x_own, xs_send.at[0])
    sent(c_own, cs_send.at[0])
    swap.wait_send()

    @pl.when(alone)
    def _():
        sent(res.at[pl.ds(0, (PARTS - 1) * sub), :], a2a_send.at[0])

    @pl.when(jnp.logical_not(alone))
    def _():
        sent(res, a2a_send.at[0])

    pltpu.make_async_copy(codes_out, codes_out, co_sem.at[0]).wait()
    pltpu.make_async_copy(rebuilt_out, rebuilt_out, ro_sem.at[0]).wait()


def deliver(codes_in, rebuilt_in, codes_out, rebuilt_out):
    codes_out[...] = codes_in[...]
    rebuilt_out[...] = rebuilt_in[...]


def per_device(residuals, enc_weight, dec_weight, enc_bias, dec_bias, active):
    rows, width = residuals.shape[1:]
    latents = enc_weight.shape[2]
    sub = rows // PARTS
    dma = pltpu.SemaphoreType.DMA

    def reduction():
        return [
            pltpu.VMEM((SLOTS, rows, width), F32),
            pltpu.VMEM((PARTS, 2, sub, width), BF16),
            pltpu.VMEM((PARTS, 2, sub, width), BF16),
            pltpu.VMEM((PARTS, 2, 2 * sub, width), BF16),
            pltpu.VMEM((PARTS, 2, 2 * sub, width), BF16),
            pltpu.VMEM((PARTS, sub, width), BF16),
            pltpu.VMEM((PARTS, sub, width), BF16),
            pltpu.VMEM((PARTS, 2, sub, width), BF16),
            pltpu.VMEM((PARTS, 2, sub, width), BF16),
            pltpu.VMEM((PARTS, sub, width), F32),
        ]

    anywhere = pl.BlockSpec(memory_space=pl.ANY)
    vmem = pl.BlockSpec(memory_space=pltpu.VMEM)
    codes, rebuilt = pl.pallas_call(
        kernel,
        out_shape=(
            jax.ShapeDtypeStruct((rows, latents), BF16),
            jax.ShapeDtypeStruct((rows, width), BF16),
        ),
        in_specs=[anywhere, anywhere, anywhere, vmem, vmem, anywhere],
        out_specs=(anywhere, anywhere),
        scratch_shapes=[pltpu.VMEM((PARTS, rows, width), BF16)] * 4
        + [pltpu.VMEM((width, width), BF16)] * 4
        + [pltpu.VMEM((rows, width), jnp.int32), pltpu.VMEM((PARTS, sub, width), BF16)]
        + reduction()
        + reduction()
        + [dma((1,)), dma((PARTS,)), dma((4,)), dma((2,))]
        + [dma((1,)), dma((PARTS, 4))] * 2
        + [dma((1,)), dma((PARTS,))] * 2
        + [dma((1,)), dma((PARTS, 4))] * 2
        + [dma((1,)), dma((1,))],
        compiler_params=pltpu.CompilerParams(
            collective_id=0, has_side_effects=True, vmem_limit_bytes=60 * 1024 * 1024
        ),
    )(
        residuals[0], enc_weight[0], dec_weight[0],
        enc_bias.reshape(1, latents), dec_bias, active,
    )
    codes, rebuilt = pl.pallas_call(
        deliver,
        out_shape=(
            jax.ShapeDtypeStruct(codes.shape, BF16),
            jax.ShapeDtypeStruct(rebuilt.shape, BF16),
        ),
        grid=(2,),
        in_specs=[pl.BlockSpec((rows // 2, latents), lambda i: (i, 0)), pl.BlockSpec((rows // 2, width), lambda i: (i, 0))],
        out_specs=(pl.BlockSpec((rows // 2, latents), lambda i: (i, 0)), pl.BlockSpec((rows // 2, width), lambda i: (i, 0))),
    )(codes, rebuilt)
    return codes, rebuilt[None]


def solution(mesh):
    return jax.shard_map(
        per_device,
        mesh=mesh,
        in_specs=(
            P("src", "tok", "lat"),
            P("src", "tok", "lat"),
            P("src", "lat", "tok"),
            P("lat"),
            P("src", "tok"),
            P("tok", "lat"),
        ),
        out_specs=(P("tok", "lat"), P("src", "lat", "tok")),
        check_vma=False,
    )
```

```python
import jax
import jax.numpy as jnp
from jax import lax
from jax.experimental import pallas as pl
from jax.experimental.pallas import tpu as pltpu
from jax.sharding import PartitionSpec as P

PARTS = 8
SLOTS = 6
PAIR_FIRST = (5, 7)
LAT_FIRST = ()
PAIR_LAST = ()
RING = 4
BF16 = jnp.bfloat16
F32 = jnp.float32


class Group:
    def __init__(self, axis):
        self.axis = axis
        self.me = lax.axis_index(axis)
        self.ring = self.me // 2
        self.half = self.me % 2
        self.right = self.at(1, self.half)
        self.left = self.at(3, self.half)
        self.partner = self.at(0, 1 - self.half)

    def at(self, step, half):
        return 2 * ((self.ring + step) % RING) + half

    def neighbours(self):
        return [{self.axis: self.right}, {self.axis: self.left}, {self.axis: self.partner}]


def either(q, chunks, special, usual):
    if not chunks:
        usual(q)
        return
    named = q == chunks[0]
    for chunk in chunks[1:]:
        named = named | (q == chunk)

    @pl.when(named)
    def _():
        special(q)

    @pl.when(jnp.logical_not(named))
    def _():
        usual(q)


class Gather:
    def __init__(self, group, buf, send, recv, sub, pair_last=()):
        self.group, self.buf, self.send, self.recv, self.sub = group, buf, send, recv, sub
        self.pair_last = pair_last

    def copy(self, q, block, sem, to, skip=0, rows=None):
        rows = rows or self.sub
        start = pl.multiple_of(block * self.sub + skip, rows)
        place = self.buf.at[q, pl.ds(start, rows), :]
        return pltpu.make_async_remote_copy(
            place, place, self.send.at[0], self.recv.at[q, sem], device_id={self.group.axis: to}
        )

    def first(self, q):
        g = self.group
        self.copy(q, g.me, 0, g.right).start()
        either(
            q, self.pair_last,
            lambda q: self.copy(q, g.me, 1, g.left).start(),
            lambda q: self.copy(q, g.me, 3, g.left).start(),
        )
        either(
            q, self.pair_last,
            lambda q: self.copy(q, g.me, 3, g.partner).start(),
            lambda q: self.copy(q, g.me, 1, g.partner).start(),
        )

    def pass_left(self, q):
        g = self.group
        self.copy(q, g.left, 0, g.right).wait_recv()

        def special(q):
            self.copy(q, g.left, 2, g.right, 0, self.sub // 2).start()
            self.copy(q, g.left, 3, g.partner).start()

        either(q, self.pair_last, special, lambda q: self.copy(q, g.left, 3, g.right).start())

    def pass_other(self, q):
        g = self.group

        def special(q):
            self.copy(q, g.right, 1, g.left).wait_recv()
            self.copy(q, g.right, 2, g.left, self.sub // 2, self.sub // 2).start()
            self.copy(q, g.right, 3, g.partner).start()

        def usual(q):
            self.copy(q, g.partner, 1, g.partner).wait_recv()
            self.copy(q, g.partner, 2, g.left).start()
            self.copy(q, g.partner, 3, g.right).start()

        either(q, self.pair_last, special, usual)

    def pass_far(self, q):
        g = self.group

        def special(q):
            self.copy(q, g.at(2, g.half), 2, g.right).wait_recv()
            self.copy(q, g.at(2, g.half), 3, g.partner).start()

        def usual(q):
            self.copy(q, g.at(1, 1 - g.half), 2, g.right).wait_recv()
            self.copy(q, g.at(1, 1 - g.half), 3, g.left).start()

        either(q, self.pair_last, special, usual)

    def last(self, q):
        rest = self.buf.at[q, pl.ds(0, 4 * self.sub), :]
        pltpu.make_async_remote_copy(
            rest, rest, self.send.at[0], self.recv.at[q, 3], device_id={self.group.axis: self.group.right}
        ).wait_recv()


class Scatter:
    def __init__(self, group, sums, place, out1, in1, out2, in2, out3, in3, out4, in4, keep, send, recv, sub, pair_first=()):
        self.group, self.sums, self.place = group, sums, place
        self.out1, self.in1, self.out2, self.in2 = out1, in1, out2, in2
        self.out3, self.in3, self.out4, self.in4, self.keep = out3, in3, out4, in4, keep
        self.send, self.recv, self.sub, self.pair_first = send, recv, sub, pair_first

    def rows(self, q, owner):
        start = pl.multiple_of(self.place(q, owner) * self.sub, self.sub)
        return (q % SLOTS, pl.ds(start, self.sub), slice(None))

    def copy(self, q, src, dst, sem, to):
        return pltpu.make_async_remote_copy(
            src, dst, self.send.at[0], self.recv.at[q, sem], device_id={self.group.axis: to}
        )

    def side(self, q, side):
        to = (self.group.right, self.group.left)[side]
        return self.copy(q, self.out1.at[q, side], self.in1.at[q, side], side, to)

    def near(self, q, side):
        to = (self.group.right, self.group.left)[side]
        rows = pl.ds(0, self.sub // 2)
        return self.copy(q, self.out1.at[q, side, rows, :], self.in1.at[q, side, rows, :], side, to)

    def double(self, q):
        return self.copy(q, self.out2.at[q], self.in2.at[q], 2, self.group.partner)

    def single(self, q):
        return self.copy(q, self.out3.at[q], self.in3.at[q], 3, self.group.partner)

    def first(self, q):
        g, sub = self.group, self.sub

        def special(q):
            for step in range(RING):
                at = slice((step % 2) * sub, (step % 2 + 1) * sub)
                self.out2[q, step // 2, at, :] = self.sums[self.rows(q, g.at(step, 1 - g.half))].astype(BF16)
            self.double(q).start()

        def usual(q):
            for h in (0, 1):
                self.out1[q, h] = self.sums[self.rows(q, g.at(2, h))].astype(BF16)
                self.side(q, h).start()

        either(q, self.pair_first, special, usual)

    def second(self, q):
        g, sub = self.group, self.sub

        def special(q):
            self.double(q).wait_recv()
            for step in (2, 1, 3, 0):
                at = slice((step % 2) * sub, (step % 2 + 1) * sub)
                value = self.sums[self.rows(q, g.at(step, g.half))] + self.in2[q, step // 2, at, :].astype(F32)
                if step == 2:
                    for side in (0, 1):
                        part = slice(side * sub // 2, (side + 1) * sub // 2)
                        self.out1[q, side, 0:sub // 2, :] = value[part].astype(BF16)
                        self.near(q, side).start()
                elif step == 0:
                    self.keep[q] = value
                else:
                    self.sums[self.rows(q, g.at(step, g.half))] = value

        def usual(q):
            for side, step in ((0, 1), (1, 3)):
                self.side(q, side).wait_recv()
                for h in (0, 1):
                    value = self.sums[self.rows(q, g.at(step, h))]
                    if h == side:
                        value = value + self.in1[q, side].astype(F32)
                    self.out2[q, side, h * sub:(h + 1) * sub, :] = value.astype(BF16)
                to = (g.right, g.left)[side]
                self.copy(q, self.out2.at[q, side], self.in2.at[q, side], 2, to).start()

        either(q, self.pair_first, special, usual)

    def third(self, q):
        g, sub = self.group, self.sub

        def special(q):
            for side, step in ((0, 1), (1, 3)):
                self.near(q, side).wait_recv()
                value = self.sums[self.rows(q, g.at(step, g.half))]
                part = slice(side * sub // 2, (side + 1) * sub // 2)
                rest = slice((1 - side) * sub // 2, (2 - side) * sub // 2)
                relayed = value[part] + self.in1[q, side, 0:sub // 2, :].astype(F32)
                self.out4[q, side, part, :] = relayed.astype(BF16)
                self.out4[q, side, rest, :] = value[rest].astype(BF16)
                to = (g.right, g.left)[side]
                self.copy(q, self.out4.at[q, side], self.in4.at[q, side], 3, to).start()

        def usual(q):
            self.copy(q, self.out2.at[q], self.in2.at[q], 2, g.right).wait_recv()

            def total(h):
                rows = pl.ds(pl.multiple_of(h * sub, sub), sub)
                return (
                    self.sums[self.rows(q, g.at(0, h))]
                    + self.in2[q, 0, rows, :].astype(F32)
                    + self.in2[q, 1, rows, :].astype(F32)
                )

            self.out3[q] = total(1 - g.half).astype(BF16)
            self.single(q).start()
            self.keep[q] = total(g.half)

        either(q, self.pair_first, special, usual)

    def last(self, q):
        def special(q):
            self.copy(q, self.out4.at[q], self.in4.at[q], 3, self.group.right).wait_recv()
            self.keep[q] += self.in4[q, 0].astype(F32) + self.in4[q, 1].astype(F32)

        def usual(q):
            self.single(q).wait_recv()
            self.keep[q] += self.in3[q].astype(F32)

        either(q, self.pair_first, special, usual)
        return self.keep[q]


def product(a, a_other, w, w_other, sums, q, arrived):
    cols = sums.shape[2]
    tile = 256
    for part in range(cols // tile):
        at = slice(part * tile, (part + 1) * tile)
        sums[q % SLOTS, :, at] = jnp.dot(a[q], w[:, at], preferred_element_type=F32)
    arrived()
    for part in range(cols // tile):
        at = slice(part * tile, (part + 1) * tile)
        sums[q % SLOTS, :, at] += jnp.dot(a_other[q], w_other[:, at], preferred_element_type=F32)


def kernel(
    res, encw, decw, encb, decb, active,
    codes_out, rebuilt_out,
    x_own, x_sib, c_own, c_sib, we_own, we_sib, wd_own, wd_sib, mask, made,
    e_sums, e_out1, e_in1, e_out2, e_in2, e_out3, e_in3, e_out4, e_in4, e_keep,
    d_sums, d_out1, d_in1, d_out2, d_in2, d_out3, d_in3, d_out4, d_in4, d_keep,
    a2a_send, a2a_recv, local_sem, wx_sem,
    xg_send, xg_recv, cg_send, cg_recv,
    xs_send, xs_recv, cs_send, cs_recv,
    er_send, er_recv, dr_send, dr_recv, co_sem, ro_sem,
):
    tok, lat, core = Group("tok"), Group("lat"), lax.axis_index("src")
    t, l = tok.me, lat.me
    sibling = {"src": 1 - core}
    width = x_own.shape[2]
    sub = x_own.shape[1] // PARTS
    alone = t == l

    def half(which):
        return pl.ds(pl.multiple_of(which * width, width), width)

    def block(index):
        return pl.ds(pl.multiple_of(index * sub, sub), sub)

    loads = [
        pltpu.make_async_copy(encw.at[:, half(core)], we_own, local_sem.at[0]),
        pltpu.make_async_copy(decw.at[half(core), :], wd_own, local_sem.at[1]),
        pltpu.make_async_copy(decw.at[half(1 - core), :], wd_sib, local_sem.at[2]),
        pltpu.make_async_copy(active.at[:, half(core)], mask, local_sem.at[3]),
    ]
    for load in loads:
        load.start()

    barrier = pltpu.get_barrier_semaphore()
    for device in tok.neighbours() + lat.neighbours() + [sibling]:
        pl.semaphore_signal(barrier, inc=1, device_id=device)

    @pl.loop(0, PARTS)
    def _(i):
        @pl.when(jnp.logical_not(alone & (i == t)))
        def _():
            pl.semaphore_signal(barrier, inc=1, device_id={"tok": i, "lat": t})

    pl.semaphore_wait(barrier, jnp.where(alone, 14, 15))

    def relay(q):
        j = (t - q + PARTS) % PARTS
        return pltpu.make_async_remote_copy(
            res.at[block(j), :], x_own.at[q, block(j), :], a2a_send.at[0], a2a_recv.at[q],
            device_id={"tok": l, "lat": j},
        )

    def stay():
        return pltpu.make_async_copy(res.at[block(l), :], x_own.at[0, block(l), :], a2a_recv.at[0])

    @pl.loop(0, PARTS)
    def _(q):
        own = alone & (q == 0)

        @pl.when(own)
        def _():
            stay().start()

        @pl.when(jnp.logical_not(own))
        def _():
            relay(q).start()

    def landed(q):
        own = alone & (q == 0)
        place = x_own.at[q, block(l), :]

        @pl.when(own)
        def _():
            stay().wait()

        @pl.when(jnp.logical_not(own))
        def _():
            pltpu.make_async_remote_copy(
                place, place, a2a_send.at[0], a2a_recv.at[q], device_id=sibling
            ).wait_recv()

    swap = pltpu.make_async_remote_copy(
        encw.at[:, half(1 - core)], we_sib, wx_sem.at[0], wx_sem.at[1], device_id=sibling
    )
    swap.start()

    xg = Gather(lat, x_own, xg_send, xg_recv, sub)
    cg = Gather(tok, c_own, cg_send, cg_recv, sub, PAIR_LAST)
    er = Scatter(
        tok, e_sums, lambda q, owner: (owner - q + PARTS) % PARTS,
        e_out1, e_in1, e_out2, e_in2, e_out3, e_in3, e_out4, e_in4, e_keep, er_send, er_recv, sub, PAIR_FIRST,
    )
    dr = Scatter(
        lat, d_sums, lambda q, owner: owner,
        d_out1, d_in1, d_out2, d_in2, d_out3, d_in3, d_out4, d_in4, d_keep, dr_send, dr_recv, sub, LAT_FIRST,
    )

    def x_swap(q):
        return pltpu.make_async_remote_copy(
            x_own.at[q], x_sib.at[q], xs_send.at[0], xs_recv.at[q], device_id=sibling
        )

    def c_swap(q):
        return pltpu.make_async_remote_copy(
            c_own.at[q], c_sib.at[q], cs_send.at[0], cs_recv.at[q], device_id=sibling
        )

    def codes_copy(q, which):
        rows = block((t - q + PARTS) % PARTS)
        src = c_sib if which else c_own
        col = (1 - core) if which else core
        return pltpu.make_async_copy(
            src.at[q, block(t), :], codes_out.at[rows, half(col)], co_sem.at[0]
        )

    def rebuilt_copy(q):
        rows = block((l - q + PARTS) % PARTS)
        return pltpu.make_async_copy(made.at[q], rebuilt_out.at[rows, :], ro_sem.at[0])

    def x_first(q):
        landed(q)
        xg.first(q)

    def x_last(q):
        xg.last(q)
        x_swap(q).start()

    def encode(q):
        @pl.when(q == 0)
        def _():
            loads[0].wait()
            swap.wait_recv()

        product(x_own, x_sib, we_own, we_sib, e_sums, q, lambda: x_swap(q).wait_recv())
        er.first(q)

    def activate(q):
        @pl.when(q == 0)
        def _():
            loads[3].wait()

        value = er.last(q) + encb[:, half(core)]
        kept = mask[block((t - q + PARTS) % PARTS), :] == 1
        c_own[q, block(t), :] = jnp.where(kept, jnp.maximum(value, 0.0), 0.0).astype(BF16)
        cg.first(q)
        codes_copy(q, 0).start()

    def c_last(q):
        cg.last(q)
        c_swap(q).start()

    def decode(q):
        @pl.when(q == 0)
        def _():
            loads[1].wait()
            loads[2].wait()

        product(c_own, c_sib, wd_own, wd_sib, d_sums, q, lambda: c_swap(q).wait_recv())
        dr.first(q)
        codes_copy(q, 1).start()

    def finish(q):
        made[q] = (dr.last(q) + decb[...]).astype(BF16)
        rebuilt_copy(q).start()

    steps = [
        (c_last, 12),
        (dr.second, 14),
        (cg.pass_left, 10),
        (decode, 12),
        (er.second, 6),
        (er.third, 7),
        (cg.pass_other, 9),
        (cg.pass_far, 10),
        (activate, 8),
        (encode, 4),
        (xg.pass_left, 2),
        (xg.pass_other, 1),
        (finish, 17),
        (xg.pass_far, 2),
        (x_first, 0),
        (dr.third, 15),
        (x_last, 3),
    ]
    rounds = PARTS + max(lag for _, lag in steps)

    @pl.loop(0, rounds)
    def _(i):
        for step, lag in steps:
            q = i - lag

            @pl.when((q >= 0) & (q < PARTS))
            def _(step=step, q=q):
                step(q)

    def sent(src, sem):
        pltpu.make_async_remote_copy(src, src, sem, a2a_recv.at[0], device_id=sibling).wait_send()

    most = pl.ds(0, PARTS - 1)
    for sem in (xg_send, cg_send, er_send, dr_send):
        sent(x_own.at[most], sem.at[0])
    sent(x_own, xs_send.at[0])
    sent(c_own, cs_send.at[0])
    swap.wait_send()

    @pl.when(alone)
    def _():
        sent(res.at[pl.ds(0, (PARTS - 1) * sub), :], a2a_send.at[0])

    @pl.when(jnp.logical_not(alone))
    def _():
        sent(res, a2a_send.at[0])

    pltpu.make_async_copy(codes_out, codes_out, co_sem.at[0]).wait()
    pltpu.make_async_copy(rebuilt_out, rebuilt_out, ro_sem.at[0]).wait()


def deliver(codes_in, rebuilt_in, codes_out, rebuilt_out):
    codes_out[...] = codes_in[...]
    rebuilt_out[...] = rebuilt_in[...]


def per_device(residuals, enc_weight, dec_weight, enc_bias, dec_bias, active):
    rows, width = residuals.shape[1:]
    latents = enc_weight.shape[2]
    sub = rows // PARTS
    dma = pltpu.SemaphoreType.DMA

    def reduction():
        return [
            pltpu.VMEM((SLOTS, rows, width), F32),
            pltpu.VMEM((PARTS, 2, sub, width), BF16),
            pltpu.VMEM((PARTS, 2, sub, width), BF16),
            pltpu.VMEM((PARTS, 2, 2 * sub, width), BF16),
            pltpu.VMEM((PARTS, 2, 2 * sub, width), BF16),
            pltpu.VMEM((PARTS, sub, width), BF16),
            pltpu.VMEM((PARTS, sub, width), BF16),
            pltpu.VMEM((PARTS, 2, sub, width), BF16),
            pltpu.VMEM((PARTS, 2, sub, width), BF16),
            pltpu.VMEM((PARTS, sub, width), F32),
        ]

    anywhere = pl.BlockSpec(memory_space=pl.ANY)
    vmem = pl.BlockSpec(memory_space=pltpu.VMEM)
    codes, rebuilt = pl.pallas_call(
        kernel,
        out_shape=(
            jax.ShapeDtypeStruct((rows, latents), BF16),
            jax.ShapeDtypeStruct((rows, width), BF16),
        ),
        in_specs=[anywhere, anywhere, anywhere, vmem, vmem, anywhere],
        out_specs=(anywhere, anywhere),
        scratch_shapes=[pltpu.VMEM((PARTS, rows, width), BF16)] * 4
        + [pltpu.VMEM((width, width), BF16)] * 4
        + [pltpu.VMEM((rows, width), jnp.int32), pltpu.VMEM((PARTS, sub, width), BF16)]
        + reduction()
        + reduction()
        + [dma((1,)), dma((PARTS,)), dma((4,)), dma((2,))]
        + [dma((1,)), dma((PARTS, 4))] * 2
        + [dma((1,)), dma((PARTS,))] * 2
        + [dma((1,)), dma((PARTS, 4))] * 2
        + [dma((1,)), dma((1,))],
        compiler_params=pltpu.CompilerParams(
            collective_id=0, has_side_effects=True, vmem_limit_bytes=60 * 1024 * 1024
        ),
    )(
        residuals[0], enc_weight[0], dec_weight[0],
        enc_bias.reshape(1, latents), dec_bias, active,
    )
    codes, rebuilt = pl.pallas_call(
        deliver,
        out_shape=(
            jax.ShapeDtypeStruct(codes.shape, BF16),
            jax.ShapeDtypeStruct(rebuilt.shape, BF16),
        ),
        grid=(2,),
        in_specs=[pl.BlockSpec((rows // 2, latents), lambda i: (i, 0)), pl.BlockSpec((rows // 2, width), lambda i: (i, 0))],
        out_specs=(pl.BlockSpec((rows // 2, latents), lambda i: (i, 0)), pl.BlockSpec((rows // 2, width), lambda i: (i, 0))),
    )(codes, rebuilt)
    return codes, rebuilt[None]


def solution(mesh):
    return jax.shard_map(
        per_device,
        mesh=mesh,
        in_specs=(
            P("src", "tok", "lat"),
            P("src", "tok", "lat"),
            P("src", "lat", "tok"),
            P("lat"),
            P("src", "tok"),
            P("tok", "lat"),
        ),
        out_specs=(P("tok", "lat"), P("src", "lat", "tok")),
        check_vma=False,
    )
```
